128 devices in a mesh: vp: 16 (over z, y), op: 8 (over x, core).
Axes of the slice: x: 4, y: 4, z: 4, core: 2. Of those that a mesh axis runs over, the one named last changes fastest.
Arguments:
- amplitudes: bfloat16 [16384, 16384], P('vp', 'op'), may hold values from -6 to 6
- integrals: bfloat16 [16, 16384, 2048], P('vp', 'op'), may hold values from -0.046875 to 0.046875
- pair_class: int32 [16384, 1], P('vp'), may hold values from 0 to 15; in each aligned block of 1024 rows (0 to 1023, 1024 to 2047, ...) at most 160 rows name the same one
Outputs:
- ladder: bfloat16 [2048, 16384], P('op', 'vp')
The draws below stay inside these ranges and needn't reach their ends.
Inputs may be any that keep to these rules, and one draw needn't show every extreme that they name: `pair_class`: in each aligned block of 1024 rows (the rows of one index of vp) no class is named by more than 160 rows; some class is named by exactly 160 rows of some block.
All inputs are finite; a program needn't handle non-finite values.
Results may differ from the reference program's by a relative error of at most 0.017.
Values may be sent and summed in bfloat16 or wider, within the bound.
No kernel may reach another device: no remote copies, remote signals or barrier semaphores. Data moves between devices by JAX's collectives and lax.ppermute only.
A program may use at most 64 MiB of HBM per device.

```python
import math
import jax
import jax.numpy as jnp
import numpy as np
from jax import lax

CD = 16384
AB = 2048
ROWS_DEV = 1024
CAP = 160
CLASSES = 16
PAIRS = 16384
N_VP = 16
N_OP = 8


def steps_of(own_key, shape, shards, low, high):
    def one(position, shards_of):
        steps = jax.random.uniform(jax.random.fold_in(jax.random.fold_in(own_key, 6), position), (shards_of,), jnp.float32, low / len(shards), high / len(shards))
        return jnp.repeat(jnp.exp(steps), shape[position] // shards_of).reshape((-1,) + (1,) * (len(shape) - position - 1))

    factor_of = one(*shards[0])
    for cut in shards[1:]:
        factor_of = factor_of * one(*cut)
    return factor_of


def assign_block(stream_key, own, number, rows, number_of, top, reach, skew):
    order = jax.random.permutation(stream_key, number_of)
    packed, usual = shares(number_of, rows * top, reach, skew, True), shares(number_of, rows * top, reach, skew, False)
    places = jnp.arange(number_of)

    def named(sizes, rotation):
        used = int((sizes > 0).sum())
        fixed = max(1, used // 4)
        passed = fixed + (places - fixed + rotation * (used - fixed)) % max(1, number_of - fixed)
        return jnp.zeros((number_of,), jnp.int32).at[order[jnp.where(places < fixed, places, passed)]].set(jnp.asarray(sizes, jnp.int32))

    sizes = jnp.where(number % 4 == 0, named(packed, number // 4), named(usual, number - number // 4 - 1))
    mixed = jax.random.permutation(jax.random.fold_in(own, 3), number_of)
    source_of, sink = mixed[0:number_of // 2 * 2:2], mixed[1:number_of // 2 * 2:2]
    slack = jnp.minimum(sizes[source_of] - 1, reach - sizes[sink]) // 2
    slack = jnp.where((source_of == order[0]) | (sink == order[0]) | (sizes[sink] == 0), 0, jnp.maximum(slack, 0))
    passed = jax.random.randint(jax.random.fold_in(own, 4), (number_of // 2,), 0, 1 << 20) % (slack + 1)
    sizes = sizes.at[source_of].add(-passed).at[sink].add(passed)
    members = jnp.searchsorted(jnp.cumsum(sizes), jnp.arange(rows * top), side="right").astype(jnp.int32)
    table = members.reshape(top, rows).T
    table = table[jax.random.permutation(jax.random.fold_in(own, 1), rows)]
    rotation = jax.random.randint(jax.random.fold_in(own, 2), (rows, 1), 0, top)
    return jnp.take_along_axis(table, (jnp.arange(top)[None, :] + rotation) % top, axis=1)


def shares(count, total, limit, lean, full):
    portions = [(1 << 20) // math.isqrt(standing ** lean) + 1 for standing in range(1, count + 1)]
    largest = limit if full else min(limit, max(-(-total // count), total * portions[0] // sum(portions)))
    least = 1 if total - largest >= count - 1 else 0
    counts, rest = [largest] + [least] * (count - 1), total - largest - least * (count - 1)
    while rest > 0:
        movable = [i for i in range(1, count) if counts[i] < largest] or [i for i in range(1, count) if counts[i] < limit]
        mass, remaining = sum([portions[i] for i in movable]), rest
        for i in movable:
            extra = min(limit - counts[i], max(1, remaining * portions[i] // mass), rest)
            counts[i] = counts[i] + extra
            rest = rest - extra
    return np.array(counts)


def normal_values(stream_key, extent, width, bound, cuts=(), held_as=jnp.bfloat16):
    drawn = width * jax.random.normal(stream_key, extent, jnp.float32)
    if cuts:
        drawn = drawn * steps_of(stream_key, extent, cuts, -0.22, 0.18)
    return jnp.clip(drawn, -bound, bound).astype(held_as)


def setup_inputs(seed: int = 0) -> dict:
    key_list = jax.random.split(jax.random.key(seed), 4)
    amplitudes = normal_values(key_list[0], (PAIRS, CD), 1.0, 6.0, ((0, 16), (1, 8)))
    integrals = normal_values(key_list[1], (CLASSES, CD, AB), CD ** -0.5, 0.046875, ((0, 16), (1, 8)))
    pair_class_keys = jax.random.split(jax.random.fold_in(key_list[2], 1), PAIRS // ROWS_DEV)
    pair_class_turns = jax.random.permutation(jax.random.fold_in(key_list[2], 3), PAIRS // ROWS_DEV)
    pair_class = jax.vmap(lambda own, number: assign_block(jax.random.fold_in(key_list[2], 2), own, number, ROWS_DEV, CLASSES, 1, CAP, 2))(pair_class_keys, pair_class_turns).reshape((PAIRS, 1))
    return dict(amplitudes=amplitudes, integrals=integrals, pair_class=pair_class)


def class_block(amplitudes, integrals, pair_class, class_id):
    others = (pair_class[:, 0] != class_id).astype(jnp.int32)
    row_order = jnp.argsort(others, stable=True)[: N_VP * CAP].astype(jnp.int32)
    usable = (pair_class[row_order, 0] == class_id).astype(jnp.float32)
    gathered = amplitudes[row_order].astype(jnp.float32).reshape(N_VP * CAP, N_OP, CD // N_OP)
    weights = lax.dynamic_index_in_dim(integrals, class_id, 0, keepdims=False)
    weights = weights.astype(jnp.float32).reshape(N_OP, CD // N_OP, AB)
    pieces = jnp.einsum("rok,oka->ora", gathered, weights)
    rounded = lax.optimization_barrier(pieces.astype(jnp.bfloat16)).astype(jnp.float32)
    summed = jnp.sum(rounded, axis=0)
    return row_order, summed * usable[:, None]


def reference(amplitudes, integrals, pair_class):
    def single_class(class_id):
        return class_block(amplitudes, integrals, pair_class, class_id)

    row_order, summed = lax.map(single_class, jnp.arange(CLASSES, dtype=jnp.int32))
    combined = jnp.zeros((PAIRS, AB), jnp.float32)
    combined = combined.at[row_order.reshape(-1)].add(summed.reshape(-1, AB))
    return combined.T.astype(jnp.bfloat16)
```

```python
import jax
import jax.numpy as jnp
from jax import lax
from jax.sharding import PartitionSpec as P

CHUNKS = (32, 32, 32, 32, 32)


def row_positions(classes, n_class):
    rows = classes.shape[1]
    onehot = (classes == lax.broadcasted_iota(jnp.int32, (n_class, rows), 0)).astype(jnp.bfloat16)
    upto = (
        lax.broadcasted_iota(jnp.int32, (rows, rows), 0)
        <= lax.broadcasted_iota(jnp.int32, (rows, rows), 1)
    ).astype(jnp.bfloat16)
    before = jnp.dot(onehot, upto, preferred_element_type=jnp.float32)
    position = jnp.sum(before * onehot.astype(jnp.float32), axis=0, keepdims=True)
    return position.astype(jnp.int32) - 1


def local(amplitudes, integrals, pair_class):
    n_class = lax.axis_size("vp")
    n_op = lax.axis_size("op")
    rows, depth = amplitudes.shape
    w = integrals[0]
    ab = w.shape[1]
    classes = pair_class.reshape(1, rows)
    position = row_positions(classes, n_class)
    out = jnp.zeros((ab // n_op, rows), jnp.float32)
    first = 0
    for size in CHUNKS:
        slot = jnp.where(
            (position >= first) & (position < first + size), classes * size + position - first, -1
        )
        pick = (slot == lax.broadcasted_iota(jnp.int32, (n_class * size, rows), 0)).astype(jnp.bfloat16)
        sent = jnp.dot(pick, amplitudes, preferred_element_type=jnp.float32).astype(jnp.bfloat16)
        got = lax.all_to_all(
            sent.reshape(n_class, size, depth), "vp", split_axis=0, concat_axis=0, tiled=True
        )
        partial = jnp.dot(
            got.reshape(n_class * size, depth), w, preferred_element_type=jnp.float32
        ).astype(jnp.bfloat16)
        summed = lax.psum_scatter(partial, "op", scatter_dimension=1, tiled=True)
        back = lax.all_to_all(
            summed.reshape(n_class, size, ab // n_op), "vp", split_axis=0, concat_axis=0, tiled=True
        )
        out = out + lax.dot_general(
            back.reshape(n_class * size, ab // n_op), pick, (((0,), (0,)), ((), ())),
            preferred_element_type=jnp.float32,
        )
        first += size
    return out.astype(jnp.bfloat16)


def solution(mesh):
    return jax.shard_map(
        local,
        mesh=mesh,
        in_specs=(P("vp", "op"), P("vp", "op", None), P("vp", None)),
        out_specs=P("op", "vp"),
        check_vma=False,
    )
```

```python
import functools

import jax
import jax.numpy as jnp
import numpy as np
from jax import lax
from jax.experimental import pallas as pl
from jax.experimental.pallas import tpu as pltpu
from jax.sharding import PartitionSpec as P

SIDE = 4
CORES = 2
STEPS = (
    ((0, 0), (0, 0)),
    ((0, 1), (1, 0)),
    ((0, 3), (3, 0)),
    ((1, 0), (0, 1)),
    ((3, 0), (0, 3)),
    ((1, 1), (3, 3)),
    ((3, 3), (1, 1)),
    ((1, 3), (3, 1)),
    ((3, 1), (1, 3)),
    ((0, 2), (2, 0)),
    ((2, 0), (0, 2)),
    ((2, 2), (2, 2)),
    ((1, 2), (2, 1)),
    ((2, 1), (1, 2)),
    ((3, 2), (2, 3)),
    ((2, 3), (3, 2)),
)
GROUPS = (9, 5, 2)
PERMUTED = (2,)
FLIGHT = 4
WAITS = {13: 0}
PLACED = (2, 2, 4, 3, 4)
FLOPS = 1 << 20


PLACES = [
    [[ways[0] for ways in STEPS].index(own[core]) for own in STEPS] for core in range(CORES)
]


def pairs(step, n_op, backward=False):
    made = []
    for vp in range(SIDE * SIDE):
        for op in range(n_op):
            dz, dy = STEPS[step][op % CORES]
            to = ((vp // SIDE + dz) % SIDE) * SIDE + (vp % SIDE + dy) % SIDE
            made.append((vp * n_op + op, to * n_op + op))
    return [(b, a) for a, b in made] if backward else made


def row_slots(classes, capacity):
    rows = classes.shape[1]
    n_step = len(STEPS)
    vp = lax.axis_index("vp")
    table = jnp.asarray(np.array(STEPS, np.int32).transpose(1, 2, 0)[..., None])
    way = jnp.where(lax.axis_index("op") % CORES == 0, table[0], table[1])
    named = (vp // SIDE + way[0]) % SIDE * SIDE + (vp % SIDE + way[1]) % SIDE
    onehot = (classes == named).astype(jnp.bfloat16)
    upto = (
        lax.broadcasted_iota(jnp.int32, (rows, rows), 0)
        <= lax.broadcasted_iota(jnp.int32, (rows, rows), 1)
    ).astype(jnp.bfloat16)
    before = jnp.dot(onehot, upto, preferred_element_type=jnp.float32)
    base = lax.broadcasted_iota(jnp.int32, (n_step, rows), 0) * capacity
    slot = jnp.where(onehot > 0, before.astype(jnp.int32) - 1 + base, 0)
    return jnp.sum(slot, axis=0, keepdims=True)


def tick_body(n_after, _, arrived, w, *refs):
    out = refs[n_after]
    out[...] = jnp.dot(
        arrived[...], w[...], preferred_element_type=jnp.float32
    ).astype(out.dtype)


def tick(arrived, w, held, place, rows, later, after):
    capacity, depth = arrived.shape
    columns = w.shape[1]
    tile = 1024
    whole = pl.BlockSpec(memory_space=pl.ANY)
    extra = [x for x in (held, later) if x is not None]
    out_specs = [pl.BlockSpec((capacity, tile), lambda i, place: (place[0], i))]
    out_shape = [jax.ShapeDtypeStruct((rows * capacity, columns), jnp.bfloat16)]
    aliases = {3: 0} if held is not None else {}
    if later is not None:
        aliases[2 + len(extra)] = 1
        out_specs.append(whole)
        out_shape.append(jax.ShapeDtypeStruct(later.shape, later.dtype))
    extra += after
    return pl.pallas_call(
        functools.partial(tick_body, len(extra)),
        grid_spec=pltpu.PrefetchScalarGridSpec(
            num_scalar_prefetch=1,
            grid=(columns // tile,),
            in_specs=[
                pl.BlockSpec((capacity, depth), lambda i, place: (0, 0)),
                pl.BlockSpec((depth, tile), lambda i, place: (0, i)),
            ] + [whole] * len(extra),
            out_specs=out_specs,
        ),
        out_shape=out_shape,
        input_output_aliases=aliases,
        compiler_params=pltpu.CompilerParams(vmem_limit_bytes=40 << 20),
        cost_estimate=pl.CostEstimate(flops=FLOPS, bytes_accessed=1 << 16, transcendentals=0),
    )(place, arrived, w, *extra)


def place_kernel(first, capacity, slot, amplitudes, *outs):
    for k, out in enumerate(outs):
        wanted = lax.broadcasted_iota(jnp.int32, (capacity, slot.shape[1]), 0) + (first + k) * capacity
        out[...] = jnp.dot(
            (slot[...] == wanted).astype(jnp.float32).astype(jnp.bfloat16), amplitudes[...],
            preferred_element_type=jnp.float32,
        ).astype(out.dtype)


def place(slot, amplitudes, first, count, capacity):
    rows, depth = amplitudes.shape
    tile = 1024
    return pl.pallas_call(
        functools.partial(place_kernel, first, capacity),
        grid=(depth // tile,),
        in_specs=[
            pl.BlockSpec(slot.shape, lambda i: (0, 0)),
            pl.BlockSpec((rows, tile), lambda i: (0, i)),
        ],
        out_specs=[pl.BlockSpec((capacity, tile), lambda i: (0, i))] * count,
        out_shape=[jax.ShapeDtypeStruct((capacity, depth), jnp.bfloat16)] * count,
        compiler_params=pltpu.CompilerParams(vmem_limit_bytes=40 << 20),
        cost_estimate=pl.CostEstimate(flops=FLOPS, bytes_accessed=1 << 16, transcendentals=0),
    )(slot, amplitudes)


def op_pairs(n_op, turn):
    made = []
    for vp in range(SIDE * SIDE):
        for op in range(n_op):
            x, core = turn(op // CORES, op % CORES)
            made.append((vp * n_op + op, vp * n_op + x % (n_op // CORES) * CORES + core))
    return made


def sum_over_op(partial, axes, n_op):
    n_x = n_op // CORES
    me = lax.axis_index("op")
    x, core = me // CORES, me % CORES
    width = partial.shape[1] // n_op
    blocks = [partial[:, b * width : (b + 1) * width] for b in range(n_op)]
    even, odd = (jnp.concatenate(blocks[c::CORES], axis=1) for c in range(CORES))
    other = lax.ppermute(
        jnp.where(core == 0, odd, even), axes, op_pairs(n_op, lambda x, c: (x, 1 - c))
    )
    both = jnp.where(core == 0, even, odd).astype(jnp.float32) + other.astype(jnp.float32)
    both = both.astype(jnp.bfloat16)

    def block(d):
        return lax.dynamic_slice_in_dim(both, (x + d) % n_x * width, width, axis=1)

    terms = [block(0)] + [
        lax.ppermute(block(d), axes, op_pairs(n_op, lambda x, c, d=d: (x + d, c)))
        for d in range(1, n_x)
    ]
    return sum(t.astype(jnp.float32) for t in terms).astype(jnp.bfloat16)


def move_kernel(capacity, order, x, out):
    for i in range(len(STEPS)):
        start = pl.multiple_of(order[i] * capacity, capacity)
        out[i * capacity : (i + 1) * capacity] = x[pl.ds(start, capacity)]


def by_owner(x, capacity):
    vp = lax.axis_index("vp")
    owner = np.arange(SIDE * SIDE)
    step_of = np.zeros((SIDE, SIDE), np.int32)
    for step, ways in enumerate(STEPS):
        step_of[ways[0]] = step
    table = np.stack([
        step_of[(me // SIDE - owner // SIDE) % SIDE, (me % SIDE - owner % SIDE) % SIDE]
        for me in range(SIDE * SIDE)
    ])
    order = lax.dynamic_slice(jnp.asarray(table), (vp, 0), (1, SIDE * SIDE)).reshape(-1)
    return pl.pallas_call(
        functools.partial(move_kernel, capacity),
        in_specs=[pl.BlockSpec(memory_space=pltpu.SMEM), pl.BlockSpec(memory_space=pltpu.VMEM)],
        out_specs=pl.BlockSpec(memory_space=pltpu.VMEM),
        out_shape=jax.ShapeDtypeStruct(x.shape, x.dtype),
    )(order, x)


def local(amplitudes, integrals, pair_class):
    axes = ("vp", "op")
    n_op = lax.axis_size("op")
    rows, depth = amplitudes.shape
    capacity = rows * 5 // 32
    w = integrals[0]
    classes = pair_class.reshape(1, rows)
    slot = row_slots(classes, capacity)

    def send(x, k):
        return lax.ppermute(x, axes, pairs(k, n_op))

    sent = [None]
    for count in PLACED:
        sent += place(slot, amplitudes, len(sent), count, capacity)
    arrived = list(place(slot, amplitudes, 0, 1, capacity))
    arrived += [send(sent[k], k) for k in range(1, 1 + FLIGHT)]
    summed, groups = [], []
    even = lax.axis_index("op") % CORES == 0
    step = 0
    for g, count in enumerate(GROUPS):
        held, first = None, step
        for row in range(count):
            after = groups[-1:] if row == 0 else []
            if step in WAITS:
                after = after + [summed[WAITS[step]]]
            later = step + FLIGHT
            place_now = jnp.where(even, PLACES[0][step] - first, PLACES[1][step] - first)
            place_now = place_now.astype(jnp.int32).reshape(1)
            if step == 0 or later >= len(STEPS):
                [held] = tick(arrived[step], w, held, place_now, count, None, after)
            else:
                held, sent[later] = tick(arrived[step], w, held, place_now, count, sent[later], after)
                arrived.append(send(sent[later], later))
            step += 1
        groups.append(held)
        if g in PERMUTED:
            summed.append(sum_over_op(held, axes, n_op))
        else:
            summed.append(lax.psum_scatter(held, "op", scatter_dimension=1, tiled=True))
    back = lax.all_to_all(
        by_owner(jnp.concatenate(summed, axis=0), capacity), "vp", split_axis=0, concat_axis=0, tiled=True
    )
    home = classes * capacity + slot % capacity
    wanted = lax.broadcasted_iota(jnp.int32, (back.shape[0], rows), 0)
    return lax.dot_general(
        back, (home == wanted).astype(jnp.bfloat16), (((0,), (0,)), ((), ())),
        preferred_element_type=jnp.float32,
    ).astype(jnp.bfloat16)


def solution(mesh):
    return jax.shard_map(
        local,
        mesh=mesh,
        in_specs=(P("vp", "op"), P("vp", "op", None), P("vp", None)),
        out_specs=P("op", "vp"),
        check_vma=False,
    )
```

```python
import functools

import jax
import jax.numpy as jnp
from jax import lax
from jax.experimental import pallas as pl
from jax.experimental.pallas import tpu as pltpu
from jax.sharding import PartitionSpec as P

CHUNKS = (112, 48)


def row_positions(classes, n_class):
    rows = classes.shape[1]
    named = classes == lax.broadcasted_iota(jnp.int32, (n_class, rows), 0)
    upto = (
        lax.broadcasted_iota(jnp.int32, (rows, rows), 0)
        <= lax.broadcasted_iota(jnp.int32, (rows, rows), 1)
    ).astype(jnp.bfloat16)
    before = jnp.dot(named.astype(jnp.bfloat16), upto, preferred_element_type=jnp.float32)
    return jnp.sum(jnp.where(named, before.astype(jnp.int32) - 1, 0), axis=0, keepdims=True)


def place_body(slot, amplitudes, out):
    size = out.shape[0]
    wanted = lax.broadcasted_iota(jnp.int32, (size, slot.shape[1]), 0) + pl.program_id(0) * size
    pick = (slot[...] == wanted).astype(jnp.float32).astype(jnp.bfloat16)
    out[...] = jnp.dot(pick, amplitudes[...], preferred_element_type=jnp.float32).astype(out.dtype)


def place(slot, amplitudes, count):
    rows, depth = amplitudes.shape
    size = 256
    return pl.pallas_call(
        place_body,
        grid=(count // size,),
        in_specs=[
            pl.BlockSpec(slot.shape, lambda i: (0, 0)),
            pl.BlockSpec((rows, depth), lambda i: (0, 0)),
        ],
        out_specs=pl.BlockSpec((size, depth), lambda i: (i, 0)),
        out_shape=jax.ShapeDtypeStruct((count, depth), jnp.bfloat16),
        compiler_params=pltpu.CompilerParams(vmem_limit_bytes=24 << 20),
        cost_estimate=pl.CostEstimate(
            flops=2 * count * rows * depth, bytes_accessed=2 * (rows + count) * depth, transcendentals=0
        ),
    )(slot, amplitudes)


def multiply_body(x, w, out):
    out[...] = jnp.dot(x[...], w[...], preferred_element_type=jnp.float32).astype(out.dtype)


def multiply(x, w):
    count, depth = x.shape
    columns = w.shape[1]
    size = 256
    return pl.pallas_call(
        multiply_body,
        grid=(count // size,),
        in_specs=[
            pl.BlockSpec((size, depth), lambda i: (i, 0)),
            pl.BlockSpec((depth, columns), lambda i: (0, 0)),
        ],
        out_specs=pl.BlockSpec((size, columns), lambda i: (i, 0)),
        out_shape=jax.ShapeDtypeStruct((count, columns), jnp.bfloat16),
        compiler_params=pltpu.CompilerParams(vmem_limit_bytes=32 << 20),
        cost_estimate=pl.CostEstimate(
            flops=2 * count * depth * columns,
            bytes_accessed=2 * (count * (depth + columns) + depth * columns), transcendentals=0,
        ),
    )(x, w)


def local(amplitudes, integrals, pair_class):
    n_class = lax.axis_size("vp")
    rows = amplitudes.shape[0]
    w = integrals[0]
    classes = pair_class.reshape(1, rows)
    position = row_positions(classes, n_class)

    def exchange(x):
        return lax.all_to_all(x, "vp", split_axis=0, concat_axis=0, tiled=True)

    slots, summed = [], []
    first = 0
    for size in CHUNKS:
        here = (position >= first) & (position < first + size)
        slots.append(jnp.where(here, classes * size + position - first, -1))
        partial = multiply(exchange(place(slots[-1], amplitudes, n_class * size)), w)
        summed.append(lax.psum_scatter(partial, "op", scatter_dimension=1, tiled=True))
        first += size
    out = 0
    for slot, x in zip(slots, summed):
        back = exchange(x)
        pick = (slot == lax.broadcasted_iota(jnp.int32, (back.shape[0], rows), 0)).astype(jnp.bfloat16)
        out = out + lax.dot_general(
            back, pick, (((0,), (0,)), ((), ())), preferred_element_type=jnp.float32
        )
    return out.astype(jnp.bfloat16)


def solution(mesh):
    return jax.shard_map(
        local,
        mesh=mesh,
        in_specs=(P("vp", "op"), P("vp", "op", None), P("vp", None)),
        out_specs=P("op", "vp"),
        check_vma=False,
    )
```

```python
import functools

import jax
import jax.numpy as jnp
from jax import lax
from jax.experimental import pallas as pl
from jax.experimental.pallas import tpu as pltpu
from jax.sharding import PartitionSpec as P

CHUNKS = (128, 32)
CORES = 2
BLOCK = 256


def row_positions(classes, n_class):
    rows = classes.shape[1]
    named = classes == lax.broadcasted_iota(jnp.int32, (n_class, rows), 0)
    upto = (
        lax.broadcasted_iota(jnp.int32, (rows, rows), 0)
        <= lax.broadcasted_iota(jnp.int32, (rows, rows), 1)
    ).astype(jnp.bfloat16)
    before = jnp.dot(named.astype(jnp.bfloat16), upto, preferred_element_type=jnp.float32)
    return jnp.sum(jnp.where(named, before.astype(jnp.int32) - 1, 0), axis=0, keepdims=True)


def place_body(slot, amplitudes, out):
    size = out.shape[0]
    wanted = lax.broadcasted_iota(jnp.int32, (size, slot.shape[1]), 0) + pl.program_id(0) * size
    pick = (slot[...] == wanted).astype(jnp.float32).astype(jnp.bfloat16)
    out[...] = jnp.dot(pick, amplitudes[...], preferred_element_type=jnp.float32).astype(out.dtype)


def place(slot, amplitudes, count):
    rows, depth = amplitudes.shape
    size = 256
    return pl.pallas_call(
        place_body,
        grid=(count // size,),
        in_specs=[
            pl.BlockSpec(slot.shape, lambda i: (0, 0)),
            pl.BlockSpec((rows, depth), lambda i: (0, 0)),
        ],
        out_specs=pl.BlockSpec((size, depth), lambda i: (i, 0)),
        out_shape=jax.ShapeDtypeStruct((count, depth), jnp.bfloat16),
        compiler_params=pltpu.CompilerParams(vmem_limit_bytes=24 << 20),
        cost_estimate=pl.CostEstimate(
            flops=2 * count * rows * depth, bytes_accessed=2 * (rows + count) * depth, transcendentals=0
        ),
    )(slot, amplitudes)


def multiply_body(x, w, out):
    out[...] = jnp.dot(x[...], w[...], preferred_element_type=jnp.float32).astype(out.dtype)


def multiply(x, w):
    count, depth = x.shape
    columns = w.shape[1]
    size = 256
    return pl.pallas_call(
        multiply_body,
        grid=(count // size,),
        in_specs=[
            pl.BlockSpec((size, depth), lambda i: (i, 0)),
            pl.BlockSpec((depth, columns), lambda i: (0, 0)),
        ],
        out_specs=pl.BlockSpec((size, columns), lambda i: (i, 0)),
        out_shape=jax.ShapeDtypeStruct((count, columns), jnp.bfloat16),
        compiler_params=pltpu.CompilerParams(vmem_limit_bytes=56 << 20),
        cost_estimate=pl.CostEstimate(
            flops=2 * count * depth * columns,
            bytes_accessed=2 * (count * (depth + columns) + depth * columns), transcendentals=0,
        ),
    )(x, w)


def add_body(n, *refs):
    total = refs[0][...].astype(jnp.float32)
    for ref in refs[1:n]:
        total = total + ref[...].astype(jnp.float32)
    total = total.astype(jnp.bfloat16)
    width = refs[n].shape[1]
    for k, out in enumerate(refs[n:]):
        out[...] = total[:, k * width : (k + 1) * width]


def add(terms, width):
    count, columns = terms[0].shape
    return pl.pallas_call(
        functools.partial(add_body, len(terms)),
        grid=(count // BLOCK,),
        in_specs=[pl.BlockSpec((BLOCK, columns), lambda i: (i, 0))] * len(terms),
        out_specs=[pl.BlockSpec((BLOCK, width), lambda i: (i, 0))] * (columns // width),
        out_shape=[jax.ShapeDtypeStruct((count, width), jnp.bfloat16)] * (columns // width),
        compiler_params=pltpu.CompilerParams(vmem_limit_bytes=16 << 20),
    )(*terms)


def sum_over_op(partial):
    n_op = lax.axis_size("op")
    n_x = n_op // CORES
    me = lax.axis_index("op")
    width = partial.shape[1] // n_op

    def columns(core):
        blocks = [((me // CORES + d) % n_x * CORES + core) * width for d in range(n_x)]
        return jnp.concatenate([lax.dynamic_slice_in_dim(partial, b, width, 1) for b in blocks], axis=1)

    mine, other = columns(me % CORES), columns(1 - me % CORES)

    def permute(x, dx, swap):
        to = [(o // CORES + dx) % n_x * CORES + (o + swap) % CORES for o in range(n_op)]
        return lax.ppermute(x, "op", list(enumerate(to)))

    blocks = add([mine, permute(other, 0, 1)], mine.shape[1] // n_x)
    terms = [blocks[0]] + [permute(blocks[d], d, 0) for d in range(1, n_x)]
    return add(terms, blocks[0].shape[1])[0]


def local(amplitudes, integrals, pair_class):
    n_class = lax.axis_size("vp")
    rows = amplitudes.shape[0]
    w = integrals[0]
    classes = pair_class.reshape(1, rows)
    position = row_positions(classes, n_class)

    def exchange(x):
        return lax.all_to_all(x, "vp", split_axis=0, concat_axis=0, tiled=True)

    slots, summed = [], []
    first = 0
    for size in CHUNKS:
        here = (position >= first) & (position < first + size)
        slots.append(jnp.where(here, classes * size + position - first, -1))
        partial = multiply(exchange(place(slots[-1], amplitudes, n_class * size)), w)
        if first + size < sum(CHUNKS):
            summed.append(lax.psum_scatter(partial, "op", scatter_dimension=1, tiled=True))
        else:
            summed.append(sum_over_op(partial))
        first += size
    out = 0
    for slot, x in zip(slots, summed):
        back = exchange(x)
        pick = (slot == lax.broadcasted_iota(jnp.int32, (back.shape[0], rows), 0)).astype(jnp.bfloat16)
        out = out + lax.dot_general(
            back, pick, (((0,), (0,)), ((), ())), preferred_element_type=jnp.float32
        )
    return out.astype(jnp.bfloat16)


def solution(mesh):
    return jax.shard_map(
        local,
        mesh=mesh,
        in_specs=(P("vp", "op"), P("vp", "op", None), P("vp", None)),
        out_specs=P("op", "vp"),
        check_vma=False,
    )
```

```python
import functools

import jax
import jax.numpy as jnp
from jax import lax
from jax.experimental import pallas as pl
from jax.experimental.pallas import tpu as pltpu
from jax.sharding import PartitionSpec as P

CHUNKS = (128, 32)
CORES = 2
BLOCK = 256


def row_positions(classes, n_class):
    rows = classes.shape[1]
    named = classes == lax.broadcasted_iota(jnp.int32, (n_class, rows), 0)
    upto = (
        lax.broadcasted_iota(jnp.int32, (rows, rows), 0)
        <= lax.broadcasted_iota(jnp.int32, (rows, rows), 1)
    ).astype(jnp.bfloat16)
    before = jnp.dot(named.astype(jnp.bfloat16), upto, preferred_element_type=jnp.float32)
    return jnp.sum(jnp.where(named, before.astype(jnp.int32) - 1, 0), axis=0, keepdims=True)


def place_body(slot, amplitudes, out):
    size = out.shape[0]
    wanted = lax.broadcasted_iota(jnp.int32, (size, slot.shape[1]), 0) + pl.program_id(0) * size
    pick = (slot[...] == wanted).astype(jnp.float32).astype(jnp.bfloat16)
    out[...] = jnp.dot(pick, amplitudes[...], preferred_element_type=jnp.float32).astype(out.dtype)


def place(slot, amplitudes, count):
    rows, depth = amplitudes.shape
    size = 256
    return pl.pallas_call(
        place_body,
        grid=(count // size,),
        in_specs=[
            pl.BlockSpec(slot.shape, lambda i: (0, 0)),
            pl.BlockSpec((rows, depth), lambda i: (0, 0)),
        ],
        out_specs=pl.BlockSpec((size, depth), lambda i: (i, 0)),
        out_shape=jax.ShapeDtypeStruct((count, depth), jnp.bfloat16),
        compiler_params=pltpu.CompilerParams(vmem_limit_bytes=24 << 20),
        cost_estimate=pl.CostEstimate(
            flops=2 * count * rows * depth, bytes_accessed=2 * (rows + count) * depth, transcendentals=0
        ),
    )(slot, amplitudes)


def multiply_body(x, w, out):
    out[...] = jnp.dot(x[...], w[...], preferred_element_type=jnp.float32).astype(out.dtype)


def multiply(x, w):
    count, depth = x.shape
    columns = w.shape[1]
    size = 512
    return pl.pallas_call(
        multiply_body,
        grid=(count // size,),
        in_specs=[
            pl.BlockSpec((size, depth), lambda i: (i, 0)),
            pl.BlockSpec((depth, columns), lambda i: (0, 0)),
        ],
        out_specs=pl.BlockSpec((size, columns), lambda i: (i, 0)),
        out_shape=jax.ShapeDtypeStruct((count, columns), jnp.bfloat16),
        compiler_params=pltpu.CompilerParams(vmem_limit_bytes=56 << 20),
        cost_estimate=pl.CostEstimate(
            flops=2 * count * depth * columns,
            bytes_accessed=2 * (count * (depth + columns) + depth * columns), transcendentals=0,
        ),
    )(x, w)


def add_body(n, *refs):
    total = refs[0][...].astype(jnp.float32)
    for ref in refs[1:n]:
        total = total + ref[...].astype(jnp.float32)
    total = total.astype(jnp.bfloat16)
    width = refs[n].shape[1]
    for k, out in enumerate(refs[n:]):
        out[...] = total[:, k * width : (k + 1) * width]


def add(terms, width):
    count, columns = terms[0].shape
    return pl.pallas_call(
        functools.partial(add_body, len(terms)),
        grid=(count // BLOCK,),
        in_specs=[pl.BlockSpec((BLOCK, columns), lambda i: (i, 0))] * len(terms),
        out_specs=[pl.BlockSpec((BLOCK, width), lambda i: (i, 0))] * (columns // width),
        out_shape=[jax.ShapeDtypeStruct((count, width), jnp.bfloat16)] * (columns // width),
        compiler_params=pltpu.CompilerParams(vmem_limit_bytes=16 << 20),
    )(*terms)


def sum_over_op(partial):
    n_op = lax.axis_size("op")
    n_x = n_op // CORES
    me = lax.axis_index("op")
    width = partial.shape[1] // n_op

    def columns(core):
        blocks = [((me // CORES + d) % n_x * CORES + core) * width for d in range(n_x)]
        return jnp.concatenate([lax.dynamic_slice_in_dim(partial, b, width, 1) for b in blocks], axis=1)

    mine, other = columns(me % CORES), columns(1 - me % CORES)

    def permute(x, dx, swap):
        to = [(o // CORES + dx) % n_x * CORES + (o + swap) % CORES for o in range(n_op)]
        return lax.ppermute(x, "op", list(enumerate(to)))

    blocks = add([mine, permute(other, 0, 1)], mine.shape[1] // n_x)
    terms = [blocks[0]] + [permute(blocks[d], d, 0) for d in range(1, n_x)]
    return add(terms, blocks[0].shape[1])[0]


def local(amplitudes, integrals, pair_class):
    n_class = lax.axis_size("vp")
    rows = amplitudes.shape[0]
    w = integrals[0]
    classes = pair_class.reshape(1, rows)
    position = row_positions(classes, n_class)

    def exchange(x):
        return lax.all_to_all(x, "vp", split_axis=0, concat_axis=0, tiled=True)

    slots, summed = [], []
    first = 0
    for size in CHUNKS:
        here = (position >= first) & (position < first + size)
        slots.append(jnp.where(here, classes * size + position - first, -1))
        partial = multiply(exchange(place(slots[-1], amplitudes, n_class * size)), w)
        if first + size < sum(CHUNKS):
            summed.append(lax.psum_scatter(partial, "op", scatter_dimension=1, tiled=True))
        else:
            summed.append(sum_over_op(partial))
        first += size
    out = 0
    for slot, x in zip(slots, summed):
        back = exchange(x)
        pick = (slot == lax.broadcasted_iota(jnp.int32, (back.shape[0], rows), 0)).astype(jnp.bfloat16)
        out = out + lax.dot_general(
            back, pick, (((0,), (0,)), ((), ())), preferred_element_type=jnp.float32
        )
    return out.astype(jnp.bfloat16)


def solution(mesh):
    return jax.shard_map(
        local,
        mesh=mesh,
        in_specs=(P("vp", "op"), P("vp", "op", None), P("vp", None)),
        out_specs=P("op", "vp"),
        check_vma=False,
    )
```

```python
import functools

import jax
import jax.numpy as jnp
from jax import lax
from jax.experimental import pallas as pl
from jax.experimental.pallas import tpu as pltpu
from jax.sharding import PartitionSpec as P

CHUNKS = (128, 32)
CORES = 2
BLOCK = 256


def row_positions(classes, n_class):
    rows = classes.shape[1]
    named = classes == lax.broadcasted_iota(jnp.int32, (n_class, rows), 0)
    upto = (
        lax.broadcasted_iota(jnp.int32, (rows, rows), 0)
        <= lax.broadcasted_iota(jnp.int32, (rows, rows), 1)
    ).astype(jnp.bfloat16)
    before = jnp.dot(named.astype(jnp.bfloat16), upto, preferred_element_type=jnp.float32)
    return jnp.sum(jnp.where(named, before.astype(jnp.int32) - 1, 0), axis=0, keepdims=True)


def place_body(slot, amplitudes, out):
    size = out.shape[0]
    wanted = lax.broadcasted_iota(jnp.int32, (size, slot.shape[1]), 0) + pl.program_id(0) * size
    pick = (slot[...] == wanted).astype(jnp.float32).astype(jnp.bfloat16)
    out[...] = jnp.dot(pick, amplitudes[...], preferred_element_type=jnp.float32).astype(out.dtype)


def place(slot, amplitudes, count):
    rows, depth = amplitudes.shape
    size = 512
    return pl.pallas_call(
        place_body,
        grid=(count // size,),
        in_specs=[
            pl.BlockSpec(slot.shape, lambda i: (0, 0)),
            pl.BlockSpec((rows, depth), lambda i: (0, 0)),
        ],
        out_specs=pl.BlockSpec((size, depth), lambda i: (i, 0)),
        out_shape=jax.ShapeDtypeStruct((count, depth), jnp.bfloat16),
        compiler_params=pltpu.CompilerParams(vmem_limit_bytes=24 << 20),
        cost_estimate=pl.CostEstimate(
            flops=2 * count * rows * depth, bytes_accessed=2 * (rows + count) * depth, transcendentals=0
        ),
    )(slot, amplitudes)


def multiply_body(x, w, out):
    out[...] = jnp.dot(x[...], w[...], preferred_element_type=jnp.float32).astype(out.dtype)


def multiply(x, w):
    count, depth = x.shape
    columns = w.shape[1]
    size = 256
    return pl.pallas_call(
        multiply_body,
        grid=(count // size,),
        in_specs=[
            pl.BlockSpec((size, depth), lambda i: (i, 0)),
            pl.BlockSpec((depth, columns), lambda i: (0, 0)),
        ],
        out_specs=pl.BlockSpec((size, columns), lambda i: (i, 0)),
        out_shape=jax.ShapeDtypeStruct((count, columns), jnp.bfloat16),
        compiler_params=pltpu.CompilerParams(vmem_limit_bytes=56 << 20),
        cost_estimate=pl.CostEstimate(
            flops=2 * count * depth * columns,
            bytes_accessed=2 * (count * (depth + columns) + depth * columns), transcendentals=0,
        ),
    )(x, w)


def add_body(n, *refs):
    total = refs[0][...].astype(jnp.float32)
    for ref in refs[1:n]:
        total = total + ref[...].astype(jnp.float32)
    total = total.astype(jnp.bfloat16)
    width = refs[n].shape[1]
    for k, out in enumerate(refs[n:]):
        out[...] = total[:, k * width : (k + 1) * width]


def add(terms, width):
    count, columns = terms[0].shape
    return pl.pallas_call(
        functools.partial(add_body, len(terms)),
        grid=(count // BLOCK,),
        in_specs=[pl.BlockSpec((BLOCK, columns), lambda i: (i, 0))] * len(terms),
        out_specs=[pl.BlockSpec((BLOCK, width), lambda i: (i, 0))] * (columns // width),
        out_shape=[jax.ShapeDtypeStruct((count, width), jnp.bfloat16)] * (columns // width),
        compiler_params=pltpu.CompilerParams(vmem_limit_bytes=16 << 20),
    )(*terms)


def sum_over_op(partial):
    n_op = lax.axis_size("op")
    n_x = n_op // CORES
    me = lax.axis_index("op")
    width = partial.shape[1] // n_op

    def columns(core):
        blocks = [((me // CORES + d) % n_x * CORES + core) * width for d in range(n_x)]
        return jnp.concatenate([lax.dynamic_slice_in_dim(partial, b, width, 1) for b in blocks], axis=1)

    mine, other = columns(me % CORES), columns(1 - me % CORES)

    def permute(x, dx, swap):
        to = [(o // CORES + dx) % n_x * CORES + (o + swap) % CORES for o in range(n_op)]
        return lax.ppermute(x, "op", list(enumerate(to)))

    blocks = add([mine, permute(other, 0, 1)], mine.shape[1] // n_x)
    terms = [blocks[0]] + [permute(blocks[d], d, 0) for d in range(1, n_x)]
    return add(terms, blocks[0].shape[1])[0]


def local(amplitudes, integrals, pair_class):
    n_class = lax.axis_size("vp")
    rows = amplitudes.shape[0]
    w = integrals[0]
    classes = pair_class.reshape(1, rows)
    position = row_positions(classes, n_class)

    def exchange(x):
        return lax.all_to_all(x, "vp", split_axis=0, concat_axis=0, tiled=True)

    slots, summed = [], []
    first = 0
    for size in CHUNKS:
        here = (position >= first) & (position < first + size)
        slots.append(jnp.where(here, classes * size + position - first, -1))
        partial = multiply(exchange(place(slots[-1], amplitudes, n_class * size)), w)
        if first + size < sum(CHUNKS):
            summed.append(lax.psum_scatter(partial, "op", scatter_dimension=1, tiled=True))
        else:
            summed.append(sum_over_op(partial))
        first += size
    out = 0
    for slot, x in zip(slots, summed):
        back = exchange(x)
        pick = (slot == lax.broadcasted_iota(jnp.int32, (back.shape[0], rows), 0)).astype(jnp.bfloat16)
        out = out + lax.dot_general(
            back, pick, (((0,), (0,)), ((), ())), preferred_element_type=jnp.float32
        )
    return out.astype(jnp.bfloat16)


def solution(mesh):
    return jax.shard_map(
        local,
        mesh=mesh,
        in_specs=(P("vp", "op"), P("vp", "op", None), P("vp", None)),
        out_specs=P("op", "vp"),
        check_vma=False,
    )
```
